512 devices in a mesh: replica: 64 (over z_lo, y, core), tensor: 8 (over z_hi, x).
Axes of the slice: x: 4, y: 8, z: 8 (z_hi: 2, z_lo: 4; z = z_hi * 4 + z_lo), core: 2. Of those that a mesh axis runs over, the one named last changes fastest.
Arguments:
- owner: int32 [192], replicated, may hold values from 0 to 63, as said below
- qkv: bfloat16 [3, 384, 64, 2048], P(None, 'replica', None, 'tensor'), may hold values from -6 to 6
- grad_out: bfloat16 [192, 64, 3200], P('replica', 'tensor'), may hold values from -1.5 to 1.5
- w_out: bfloat16 [128, 16, 3200], P(None, 'tensor'), may hold values from -0.125 to 0.125
- layer_scale: float32 [3200], replicated, may hold values from 0.1 to 1.9
Outputs:
- grad_qkv: bfloat16 [3, 384, 64, 2048], P(None, 'replica', None, 'tensor')
- grad_w: float32 [128, 16, 3200], P('replica', 'tensor')
- grad_scale: float32 [3200], replicated
The draws below stay inside these ranges and needn't reach their ends.
Inputs may be any that keep to these rules, and one draw needn't show every extreme that they name: `owner`: image i comes from source device i // 3. At most 2 images of one source device go to one replica, and some source sends exactly 2 to one replica. A replica works on at most 6 images, some on exactly 6; every replica's count is a multiple of 3.
All inputs are finite; a program needn't handle non-finite values.
Results may differ from the reference program's by a relative error of at most 0.02.
Values may be sent and summed in bfloat16 or wider, within the bound.
No kernel may reach another device: no remote copies, remote signals or barrier semaphores. Data moves between devices by JAX's collectives and lax.ppermute only.
A program may use at most 64 MiB of HBM per device.

```python
import jax
import jax.numpy as jnp
from jax import lax

D = 3200
HEADS = 16
HD = 128
IMG_TOK = 64
IMG_SRC = 3
MOST = 6
IMAGES = 192
SLOTS = 384
N_REPLICA = 64


def draw_owner(key, part):
    key = jax.random.fold_in(key, 5)
    key_perm, key_offset, key_order = jax.random.split(key, 3)
    replicas = N_REPLICA
    per_source = IMG_SRC
    shuffled = jax.random.permutation(key_perm, replicas).astype(jnp.int32)
    first_value = shuffled[0]
    shuffled = jnp.where(shuffled == 0, first_value, shuffled)
    shuffled = shuffled.at[0].set(0)
    last_value = shuffled[replicas - 1]
    shuffled = jnp.where(shuffled == replicas - 1, last_value, shuffled)
    shuffled = shuffled.at[replicas - 1].set(replicas - 1)
    offset = jax.random.randint(key_offset, (), 0, replicas)
    ranking = jax.random.randint(key_order, (replicas, per_source), 0, 1 << 20) * per_source + jnp.arange(per_source)[None, :]
    within = jnp.argsort(ranking, axis=1)
    sources = jnp.arange(replicas)[:, None]
    position = (sources + within + offset) % replicas
    folded = jnp.where(position < replicas // 2, position // 2, position)
    return shuffled[folded].reshape(replicas * per_source).astype(jnp.int32)


def draw_qkv(key, part):
    key = jax.random.fold_in(key, 11)
    key_base = jax.random.fold_in(key, 0)
    shape = (3, SLOTS, IMG_TOK, HEADS, HD)
    slot_pos = (jnp.arange(SLOTS) // MOST).astype(jnp.float32) / max(N_REPLICA - 1, 1)
    base = jnp.clip(jax.random.normal(key_base, shape, jnp.float32), -6.0, 6.0)
    rising = 1.0 + 2.0 * slot_pos
    values = jnp.clip(base[2] * rising[:, None, None, None], -6.0, 6.0)
    queries = base[0]
    keys_in = base[1]
    stacked = jnp.stack([queries, keys_in, values])
    return stacked.reshape(3, SLOTS, IMG_TOK, HEADS * HD).astype(jnp.bfloat16)


def block_levels(own_key, dims, cuts, least, high):
    def one(dim, blocks):
        steps = jax.random.uniform(jax.random.fold_in(jax.random.fold_in(own_key, 6), dim), (blocks,), jnp.float32, least / len(cuts), high / len(cuts))
        return jnp.repeat(jnp.exp(steps), dims[dim] // blocks).reshape((-1,) + (1,) * (len(dims) - dim - 1))

    level = one(*cuts[0])
    for cut in cuts[1:]:
        level = level * one(*cut)
    return level


def bell_draw(own_key, extent, deviation, bound, pieces=(), kind=jnp.bfloat16):
    factor_of = block_levels(own_key, extent, pieces, -0.22, 0.18) if pieces else 1.0
    array = jax.random.normal(own_key, extent, jnp.float32) * deviation * factor_of
    return jnp.minimum(jnp.maximum(array, -bound), bound).astype(kind)


def setup_inputs(seed: int = 0) -> dict:
    arg_keys = jax.random.split(jax.random.key(seed), 6)
    owner = draw_owner(jax.random.fold_in(arg_keys[5], 71), 0)
    qkv = draw_qkv(jax.random.fold_in(arg_keys[5], 71), 0)
    grad_out = bell_draw(arg_keys[2], (IMAGES, IMG_TOK, D), 0.1, 1.5, ((0, 64), (1, 8)))
    w_out = bell_draw(arg_keys[3], (HD, HEADS, D), (HEADS * HD) ** -0.5, 0.125, ((1, 8),))
    layer_scale = jnp.clip(1.0 + 0.18 * jax.random.normal(arg_keys[4], (D,), jnp.float32), 0.1, 1.9)
    return dict(owner=owner, qkv=qkv, grad_out=grad_out, w_out=w_out, layer_scale=layer_scale)


def attention_backward(queries, keys_in, values, dealt, weights, layer_scale, head_size):
    factor = head_size ** -0.5
    scores = jnp.einsum('mqhe,mkhe->mhqk', queries.astype(jnp.float32), keys_in.astype(jnp.float32)) * factor
    row_peak = jnp.max(scores, axis=-1, keepdims=True)
    raised = jnp.exp(scores - row_peak)
    probs = raised / jnp.sum(raised, axis=-1, keepdims=True)
    probs_low = probs.astype(jnp.bfloat16)
    attended = jnp.einsum('mhqk,mkhe->mqhe', probs_low.astype(jnp.float32), values.astype(jnp.float32)).astype(jnp.bfloat16)
    scaled = (dealt.astype(jnp.float32) * layer_scale).astype(jnp.bfloat16)
    d_attended = jnp.einsum('mtc,ehc->mthe', scaled.astype(jnp.float32), weights.astype(jnp.float32)).astype(jnp.bfloat16)
    d_values = jnp.einsum('mhqk,mqhe->mkhe', probs_low.astype(jnp.float32), d_attended.astype(jnp.float32)).astype(jnp.bfloat16)
    d_probs = jnp.einsum('mqhe,mkhe->mhqk', d_attended.astype(jnp.float32), values.astype(jnp.float32))
    row_total = jnp.sum(probs * d_probs, axis=-1, keepdims=True)
    d_scores = (probs * (d_probs - row_total) * factor).astype(jnp.bfloat16)
    d_query = jnp.einsum('mhqk,mkhe->mqhe', d_scores.astype(jnp.float32), keys_in.astype(jnp.float32)).astype(jnp.bfloat16)
    d_keys = jnp.einsum('mhqk,mqhe->mkhe', d_scores.astype(jnp.float32), queries.astype(jnp.float32)).astype(jnp.bfloat16)
    return jnp.stack([d_query, d_keys, d_values]), attended, scaled


def reference(owner, qkv, grad_out, w_out, layer_scale):
    replica_ids = jnp.arange(N_REPLICA, dtype=jnp.int32)
    member = (owner[:, None] == replica_ids[None, :]).astype(jnp.int32)
    before = jnp.cumsum(member, axis=0) - member
    rank = jnp.sum(before * member, axis=1)
    slot_index = (owner * MOST + rank).astype(jnp.int32)
    dealt_all = jnp.zeros((SLOTS, IMG_TOK, D), jnp.bfloat16).at[slot_index].set(grad_out)

    def per_replica(totals, replica_id):
        first_slot = (replica_id * MOST).astype(jnp.int32)
        block = lax.dynamic_slice_in_dim(qkv, first_slot, MOST, 1).reshape(3, MOST, IMG_TOK, HEADS, HD)
        dealt = lax.dynamic_slice_in_dim(dealt_all, first_slot, MOST, 0)
        grads, attended, scaled = attention_backward(block[0], block[1], block[2], dealt, w_out, layer_scale, HD)
        weight_part = jnp.einsum('mthe,mtc->ehc', attended.astype(jnp.float32), scaled.astype(jnp.float32))
        projected = jnp.einsum('mthe,ehc->mtc', attended.astype(jnp.float32), w_out.astype(jnp.float32))
        scale_part = jnp.sum(dealt.astype(jnp.float32) * projected, axis=(0, 1))
        return (totals[0] + weight_part, totals[1] + scale_part), grads.reshape(3, MOST, IMG_TOK, HEADS * HD)

    start_totals = (jnp.zeros((HD, HEADS, D), jnp.float32), jnp.zeros((D,), jnp.float32))
    (grad_w, grad_scale), stacked = lax.scan(per_replica, start_totals, replica_ids)
    grad_qkv = jnp.transpose(stacked, (1, 0, 2, 3, 4)).reshape(3, SLOTS, IMG_TOK, HEADS * HD)
    return grad_qkv, grad_w, grad_scale
```

```python
import jax
import jax.numpy as jnp
from jax import lax
from jax.sharding import PartitionSpec as P

N_X = 4


def tensor_step(shift_hi, shift_x):
    pairs = []
    for index in range(8):
        high, x = index // N_X, index % N_X
        pairs.append((index, (high + shift_hi) % 2 * N_X + (x + shift_x) % N_X))
    return pairs


def deal(owner, grad_out, slot_count):
    replicas, runs = 64, 5
    images, tokens, width = grad_out.shape
    ids = jnp.arange(replicas * images, dtype=jnp.int32)
    same = (owner[:, None] == owner[None, :]) & (ids[None, :] < ids[:, None])
    slot_of = owner * slot_count + jnp.sum(same.astype(jnp.int32), axis=1)
    slots = jnp.arange(replicas * slot_count, dtype=jnp.int32)
    chosen = (slots[:, None] == slot_of[None, :]).astype(grad_out.dtype)

    pieces = grad_out.reshape(images, tokens, runs, width // runs).transpose(1, 2, 0, 3)
    pieces = pieces.reshape(tokens * runs, images, width // runs)
    pieces = jnp.pad(pieces, ((0, replicas - tokens * runs), (0, 0), (0, 0)))
    held = lax.all_to_all(pieces, "replica", 0, 0).reshape(replicas * images, width // runs)
    dealt = jnp.einsum("mi,ic->mc", chosen, held, preferred_element_type=jnp.float32)
    dealt = dealt.astype(grad_out.dtype).reshape(replicas, slot_count, width // runs)
    mine = lax.all_to_all(dealt, "replica", 0, 0)[: tokens * runs]
    mine = mine.reshape(tokens, runs, slot_count, width // runs).transpose(2, 0, 1, 3)
    return mine.reshape(slot_count, tokens, width)


def ring_gather(block):
    half = block.shape[0] // 2
    ahead, behind = tensor_step(0, 1), tensor_step(0, -1)
    from_left = lax.ppermute(block, "tensor", ahead)
    from_right = lax.ppermute(block, "tensor", behind)
    far_low = lax.ppermute(from_left[:half], "tensor", ahead)
    far_high = lax.ppermute(from_right[half:], "tensor", behind)
    return [block, from_left, from_right, jnp.concatenate([far_low, far_high])]


def gather_tokens(block):
    other = lax.ppermute(block, "tensor", tensor_step(1, 0))
    near = ring_gather(block)
    far = ring_gather(other)
    me = lax.axis_index("tensor")
    high, x = me // N_X, me % N_X
    places = []
    for hi in (high, 1 - high):
        for step in (0, -1, 1, 2):
            places.append(hi * N_X + (x + step + N_X) % N_X)
    return jnp.stack(near + far), jnp.stack(places)


def local(owner, qkv, grad_out, w_out, layer_scale):
    slots, tokens = qkv.shape[1], qkv.shape[2]
    size, heads, width = w_out.shape
    groups = 8
    run = tokens // groups
    factor = size ** (-0.5)

    dealt = deal(owner, grad_out, slots)

    block = qkv.reshape(3, slots, tokens, heads, size)
    queries, keys_in, values = block[0], block[1], block[2]
    scores = (
        jnp.einsum("mqhe,mkhe->mhqk", queries, keys_in, preferred_element_type=jnp.float32) * factor
    )
    raised = jnp.exp(scores - jnp.max(scores, axis=-1, keepdims=True))
    probs = raised / jnp.sum(raised, axis=-1, keepdims=True)
    probs_low = probs.astype(jnp.bfloat16)
    attended = jnp.einsum(
        "mhqk,mkhe->mqeh", probs_low, values, preferred_element_type=jnp.float32
    ).astype(jnp.bfloat16)
    weights = w_out.reshape(size * heads, width)
    scaled_weights = (weights.astype(jnp.float32) * layer_scale).astype(jnp.bfloat16)

    pieces, places = gather_tokens(dealt)
    grouped = attended.reshape(slots, groups, run, size * heads).transpose(1, 0, 2, 3)
    in_order = grouped[places].reshape(groups * slots * run, size * heads)
    flat = pieces.reshape(groups * slots * run, width)
    product = jnp.einsum("nw,nc->wc", in_order, flat, preferred_element_type=jnp.float32)
    partial = (product * layer_scale).astype(jnp.bfloat16)
    scale_part = jnp.sum(product * weights.astype(jnp.float32), axis=0).astype(jnp.bfloat16)

    replicas = 64
    rows = size * heads // replicas
    outgoing = jnp.concatenate(
        [
            partial.reshape(replicas, rows, width),
            jnp.broadcast_to(scale_part, (replicas, 1, width)),
        ],
        axis=1,
    )
    arrived = lax.all_to_all(outgoing, "replica", 0, 0)
    summed = jnp.sum(arrived.astype(jnp.float32), axis=0)
    grad_w = summed[:rows].reshape(size // replicas, heads, width)
    scale_copies = jnp.broadcast_to(summed[rows], (groups, width))
    grad_scale = jnp.sum(lax.all_to_all(scale_copies, "tensor", 0, 0), axis=0)

    d_flat = jnp.einsum(
        "nc,wc->nw", flat, scaled_weights, preferred_element_type=jnp.float32
    ).astype(jnp.bfloat16)
    d_grouped = d_flat.reshape(groups, slots, run, size, heads)
    back = jnp.argsort(places)
    d_attended = d_grouped[back].transpose(1, 0, 2, 4, 3).reshape(slots, tokens, heads, size)
    d_values = jnp.einsum(
        "mhqk,mqhe->mkhe", probs_low, d_attended, preferred_element_type=jnp.float32
    ).astype(jnp.bfloat16)
    d_probs = jnp.einsum("mqhe,mkhe->mhqk", d_attended, values, preferred_element_type=jnp.float32)
    row_total = jnp.sum(probs * d_probs, axis=-1, keepdims=True)
    d_scores = (probs * (d_probs - row_total) * factor).astype(jnp.bfloat16)
    d_query = jnp.einsum(
        "mhqk,mkhe->mqhe", d_scores, keys_in, preferred_element_type=jnp.float32
    ).astype(jnp.bfloat16)
    d_keys = jnp.einsum(
        "mhqk,mqhe->mkhe", d_scores, queries, preferred_element_type=jnp.float32
    ).astype(jnp.bfloat16)
    grad_qkv = jnp.stack([d_query, d_keys, d_values]).reshape(3, slots, tokens, heads * size)
    return (grad_qkv, grad_w, grad_scale)


def solution(mesh):
    in_specs = (
        P(),
        P(None, "replica", None, "tensor"),
        P("replica", "tensor", None),
        P(None, "tensor", None),
        P(),
    )
    out_specs = (P(None, "replica", None, "tensor"), P("replica", "tensor", None), P())
    return jax.shard_map(local, mesh=mesh, in_specs=in_specs, out_specs=out_specs, check_vma=False)
```

```python
import jax
import jax.numpy as jnp
from jax import lax
from jax.experimental import pallas as pl
from jax.experimental.pallas import tpu as pltpu
from jax.sharding import PartitionSpec as P

N_X = 4


def tensor_step(shift_hi, shift_x):
    pairs = []
    for index in range(8):
        high, x = index // N_X, index % N_X
        pairs.append((index, (high + shift_hi) % 2 * N_X + (x + shift_x) % N_X))
    return pairs


def deal(owner, grad_out, slot_count):
    replicas, runs = 64, 5
    images, tokens, width = grad_out.shape
    ids = jnp.arange(replicas * images, dtype=jnp.int32)
    same = (owner[:, None] == owner[None, :]) & (ids[None, :] < ids[:, None])
    slot_of = owner * slot_count + jnp.sum(same.astype(jnp.int32), axis=1)
    slots = jnp.arange(replicas * slot_count, dtype=jnp.int32)
    chosen = (slots[:, None] == slot_of[None, :]).astype(grad_out.dtype)

    pieces = grad_out.reshape(images, tokens, runs, width // runs).transpose(1, 2, 0, 3)
    pieces = pieces.reshape(tokens * runs, images, width // runs)
    pieces = jnp.pad(pieces, ((0, replicas - tokens * runs), (0, 0), (0, 0)))
    held = lax.all_to_all(pieces, "replica", 0, 0).reshape(replicas * images, width // runs)
    dealt = jnp.einsum("mi,ic->mc", chosen, held, preferred_element_type=jnp.float32)
    dealt = dealt.astype(grad_out.dtype).reshape(replicas, slot_count, width // runs)
    mine = lax.all_to_all(dealt, "replica", 0, 0)[: tokens * runs]
    mine = mine.reshape(tokens, runs, slot_count, width // runs).transpose(2, 0, 1, 3)
    return mine.reshape(slot_count, tokens, width)


def ring_gather(block):
    steps = [lax.ppermute(block, "tensor", tensor_step(0, k)) for k in (1, -1, 2)]
    return [block] + steps


def gather_tokens(block):
    other = lax.ppermute(block, "tensor", tensor_step(1, 0))
    near = ring_gather(block)
    far = ring_gather(other)
    me = lax.axis_index("tensor")
    high, x = me // N_X, me % N_X
    places = []
    for hi in (high, 1 - high):
        for step in (0, -1, 1, 2):
            places.append(hi * N_X + (x + step + N_X) % N_X)
    return jnp.stack(near + far), jnp.stack(places)


def replica_step(move):
    pairs = []
    for index in range(64):
        z, y, core = index // 16, index // 2 % 8, index % 2
        new_z, new_y, new_core = move(z, y, core)
        pairs.append((index, new_z * 16 + new_y * 2 + new_core))
    return pairs


def over_chip_and_tensor(part):
    near = [
        [(chip * 2 + core) * 8 + index for core in range(2) for index in range(8)]
        for chip in range(32)
    ]
    copies = jnp.broadcast_to(part, (16, 1) + part.shape)
    arrived = lax.all_to_all(copies, ("replica", "tensor"), 0, 0, axis_index_groups=near)
    return jnp.sum(arrived, axis=(0, 1))


def product_body(left_ref, right_ref, weight_ref, gain_ref, given_ref, kept_ref, scale_ref):
    product = jnp.dot(left_ref[...], right_ref[...], preferred_element_type=jnp.float32)
    scale_ref[...] = jnp.sum(
        product * weight_ref[...].astype(jnp.float32), axis=0, keepdims=True
    )
    partial = product * gain_ref[...]
    half = given_ref.shape[0]
    given_ref[...] = partial[:half].astype(jnp.bfloat16)
    kept_ref[...] = partial[half:]


def weight_products(left, right, weights, gain):
    rows, depth = left.shape
    width = right.shape[1]
    step = width // 5
    by_column = lambda height: pl.BlockSpec((height, step), lambda i: (0, i))
    return pl.pallas_call(
        product_body,
        grid=(5,),
        in_specs=[
            pl.BlockSpec((rows, depth), lambda i: (0, 0)),
            by_column(depth),
            by_column(rows),
            by_column(1),
        ],
        out_specs=[by_column(rows // 2), by_column(rows // 2), by_column(1)],
        out_shape=[
            jax.ShapeDtypeStruct((rows // 2, width), jnp.bfloat16),
            jax.ShapeDtypeStruct((rows // 2, width), jnp.float32),
            jax.ShapeDtypeStruct((1, width), jnp.float32),
        ],
        compiler_params=pltpu.CompilerParams(vmem_limit_bytes=24 * 2**20),
        cost_estimate=pl.CostEstimate(
            flops=2 * rows * depth * width, bytes_accessed=7 * 2**20, transcendentals=0
        ),
        name="weight_products",
    )(left, right, weights, gain)


def outgoing_body(kept_ref, taken_ref, extra_ref, out_ref):
    width = kept_ref.shape[1]
    held = out_ref.shape[1]
    total = kept_ref[...] + taken_ref[...].astype(jnp.float32)
    for block in range(out_ref.shape[0]):
        out_ref[block, :, :width] = total[block * held : (block + 1) * held].astype(jnp.bfloat16)
        out_ref[block, :, width:] = extra_ref[...]


def outgoing_blocks(kept, taken, extra):
    rows, width = kept.shape
    held, more = extra.shape
    step = 32
    by_row = pl.BlockSpec((step, width), lambda i: (i, 0))
    return pl.pallas_call(
        outgoing_body,
        grid=(rows // step,),
        in_specs=[by_row, by_row, pl.BlockSpec((held, more), lambda i: (0, 0))],
        out_specs=pl.BlockSpec((step // held, held, width + more), lambda i: (i, 0, 0)),
        out_shape=jax.ShapeDtypeStruct((rows // held, held, width + more), jnp.bfloat16),
        compiler_params=pltpu.CompilerParams(vmem_limit_bytes=24 * 2**20),
        cost_estimate=pl.CostEstimate(
            flops=rows * width, bytes_accessed=4 * 2**20, transcendentals=0
        ),
        name="outgoing_blocks",
    )(kept, taken, extra)


def local(owner, qkv, grad_out, w_out, layer_scale):
    slots, tokens = qkv.shape[1], qkv.shape[2]
    size, heads, width = w_out.shape
    groups = 8
    run = tokens // groups
    factor = size ** (-0.5)
    rows = size * heads
    core = lax.axis_index("replica") % 2

    dealt = deal(owner, grad_out, slots)

    position = jnp.arange(rows, dtype=jnp.int32)
    e_of = position % 128 // 4 * 4 + 2 * jnp.where(position < 128, 1 - core, core) + position % 4 // 2
    h_of = position % 2
    column = jnp.arange(rows, dtype=jnp.int32)
    by_head = (column[:, None] == (h_of * size + e_of)[None, :]).astype(jnp.bfloat16)
    by_size = (column[:, None] == (e_of * heads + h_of)[None, :]).astype(jnp.bfloat16)

    block = qkv.reshape(3, slots, tokens, heads, size)
    queries, keys_in, values = block[0], block[1], block[2]
    scores = (
        jnp.einsum("mqhe,mkhe->mhqk", queries, keys_in, preferred_element_type=jnp.float32) * factor
    )
    raised = jnp.exp(scores - jnp.max(scores, axis=-1, keepdims=True))
    probs = raised / jnp.sum(raised, axis=-1, keepdims=True)
    probs_low = probs.astype(jnp.bfloat16)
    attended = jnp.einsum(
        "mhqk,mkhe->mqhe", probs_low, values, preferred_element_type=jnp.float32
    ).astype(jnp.bfloat16)
    weights = jnp.einsum(
        "wp,wc->pc",
        by_size,
        w_out.reshape(rows, width),
        preferred_element_type=jnp.float32,
    )
    scaled_weights = (weights * layer_scale).astype(jnp.bfloat16)
    sent_order = jnp.einsum(
        "nw,wp->np",
        attended.reshape(slots * tokens, rows),
        by_head,
        preferred_element_type=jnp.float32,
    ).astype(jnp.bfloat16)
    grouped = sent_order.reshape(slots, groups, run, rows).transpose(1, 0, 2, 3)

    pieces, places = gather_tokens(dealt)
    in_order = grouped[places].reshape(groups * slots * run, rows)
    flat = pieces.reshape(groups * slots * run, width)
    given, kept, scale_part = weight_products(
        in_order.T, flat, weights.astype(jnp.bfloat16), layer_scale[None, :]
    )
    taken = lax.ppermute(given, "replica", replica_step(lambda z, y, c: (z, y, 1 - c)))
    columns = [
        [z * 16 + y * 2 + c for z in range(4) for y in range(8)] for c in range(2)
    ]
    held = rows // 64
    extra = over_chip_and_tensor(scale_part[0]).astype(jnp.bfloat16)
    extra = jnp.pad(extra.reshape(held, width // held), ((0, 0), (0, 96)))
    outgoing = outgoing_blocks(kept, taken, extra)
    arrived = lax.all_to_all(outgoing, "replica", 0, 0, axis_index_groups=columns)
    summed = jnp.sum(arrived.astype(jnp.float32), axis=0)
    grad_w = summed[:, :width].reshape(size // 64, heads, width)
    grad_scale = summed[:, width : width + width // held].reshape(width)

    flat, _ = lax.optimization_barrier((flat, outgoing))
    d_flat = jnp.einsum(
        "nc,wc->nw", flat, scaled_weights, preferred_element_type=jnp.float32
    ).astype(jnp.bfloat16)
    d_heads = jnp.einsum("np,wp->nw", d_flat, by_head, preferred_element_type=jnp.float32)
    d_grouped = d_heads.astype(jnp.bfloat16).reshape(groups, slots, run, rows)
    back = jnp.sum(
        jnp.where(places[None, :] == jnp.arange(groups)[:, None], jnp.arange(groups)[None, :], 0),
        axis=1,
    )
    d_attended = d_grouped[back].transpose(1, 0, 2, 3).reshape(slots, tokens, heads, size)
    d_values = jnp.einsum(
        "mhqk,mqhe->mkhe", probs_low, d_attended, preferred_element_type=jnp.float32
    ).astype(jnp.bfloat16)
    d_probs = jnp.einsum("mqhe,mkhe->mhqk", d_attended, values, preferred_element_type=jnp.float32)
    row_total = jnp.sum(probs * d_probs, axis=-1, keepdims=True)
    d_scores = (probs * (d_probs - row_total) * factor).astype(jnp.bfloat16)
    d_query = jnp.einsum(
        "mhqk,mkhe->mqhe", d_scores, keys_in, preferred_element_type=jnp.float32
    ).astype(jnp.bfloat16)
    d_keys = jnp.einsum(
        "mhqk,mqhe->mkhe", d_scores, queries, preferred_element_type=jnp.float32
    ).astype(jnp.bfloat16)
    grad_qkv = jnp.stack([d_query, d_keys, d_values]).reshape(3, slots, tokens, heads * size)
    return (grad_qkv, grad_w, grad_scale)


def solution(mesh):
    in_specs = (
        P(),
        P(None, "replica", None, "tensor"),
        P("replica", "tensor", None),
        P(None, "tensor", None),
        P(),
    )
    out_specs = (P(None, "replica", None, "tensor"), P("replica", "tensor", None), P())
    return jax.shard_map(local, mesh=mesh, in_specs=in_specs, out_specs=out_specs, check_vma=False)
```

```python
import jax
import jax.numpy as jnp
from jax import lax
from jax.experimental import pallas as pl
from jax.experimental.pallas import tpu as pltpu
from jax.sharding import PartitionSpec as P

N_X = 4


def tensor_step(shift_hi, shift_x):
    pairs = []
    for index in range(8):
        high, x = index // N_X, index % N_X
        pairs.append((index, (high + shift_hi) % 2 * N_X + (x + shift_x) % N_X))
    return pairs


def deal(owner, grad_out, slot_count):
    replicas, part, lanes = 64, 4, 128
    images, tokens, width = grad_out.shape
    parts, runs = tokens // part, width // lanes
    pieces = parts * runs
    ids = jnp.arange(replicas * images, dtype=jnp.int32)
    same = (owner[:, None] == owner[None, :]) & (ids[None, :] < ids[:, None])
    slot_of = owner * slot_count + jnp.sum(same.astype(jnp.int32), axis=1)
    padded = jnp.pad(slot_of.reshape(replicas, images), ((0, 0), (0, 1)), constant_values=-1)
    row_of = (padded[:, :, None] * part + jnp.arange(part, dtype=jnp.int32)).reshape(-1)
    rows = jnp.arange(replicas * slot_count * part, dtype=jnp.int32)
    chosen = (rows[:, None] == row_of[None, :]).astype(grad_out.dtype)

    spread = grad_out.reshape(images, parts, part, runs, lanes).transpose(3, 1, 0, 2, 4)
    spread = spread.reshape(pieces, images * part, lanes)
    spread = jnp.pad(spread, ((0, replicas - pieces), (0, part), (0, 0)))
    held = lax.all_to_all(spread, "replica", 0, 0).reshape(replicas * (images + 1) * part, lanes)
    dealt = jnp.einsum("mi,ic->mc", chosen, held, preferred_element_type=jnp.float32)
    dealt = dealt.astype(grad_out.dtype).reshape(replicas, slot_count * part, lanes)
    mine = lax.all_to_all(dealt, "replica", 0, 0)[:pieces]
    mine = mine.reshape(runs, parts, slot_count, part, lanes).transpose(2, 1, 3, 0, 4)
    return mine.reshape(slot_count, tokens, width)


def ring_gather(block):
    steps = [lax.ppermute(block, "tensor", tensor_step(0, k)) for k in (1, -1, 2)]
    return [block] + steps


def gather_tokens(block):
    other = lax.ppermute(block, "tensor", tensor_step(1, 0))
    near = ring_gather(block)
    far = ring_gather(other)
    me = lax.axis_index("tensor")
    high, x = me // N_X, me % N_X
    places = []
    for hi in (high, 1 - high):
        for step in (0, -1, 1, 2):
            places.append(hi * N_X + (x + step + N_X) % N_X)
    return jnp.stack(near + far), jnp.stack(places)


def replica_step(move):
    pairs = []
    for index in range(64):
        z, y, core = index // 16, index // 2 % 8, index % 2
        new_z, new_y, new_core = move(z, y, core)
        pairs.append((index, new_z * 16 + new_y * 2 + new_core))
    return pairs


def over_chip_and_tensor(part):
    near = [
        [(chip * 2 + core) * 8 + index for core in range(2) for index in range(8)]
        for chip in range(32)
    ]
    copies = jnp.broadcast_to(part, (16, 1) + part.shape)
    arrived = lax.all_to_all(copies, ("replica", "tensor"), 0, 0, axis_index_groups=near)
    return jnp.sum(arrived, axis=(0, 1))


def product_body(left_ref, right_ref, weight_ref, gain_ref, given_ref, kept_ref, scale_ref):
    product = jnp.dot(left_ref[...], right_ref[...], preferred_element_type=jnp.float32)
    scale_ref[...] = jnp.sum(
        product * weight_ref[...].astype(jnp.float32), axis=0, keepdims=True
    )
    partial = product * gain_ref[...]
    half = given_ref.shape[0]
    given_ref[...] = partial[:half].astype(jnp.bfloat16)
    kept_ref[...] = partial[half:].astype(jnp.bfloat16)


def weight_products(left, right, weights, gain):
    rows, depth = left.shape
    width = right.shape[1]
    step = width // 5
    by_column = lambda height: pl.BlockSpec((height, step), lambda i: (0, i))
    return pl.pallas_call(
        product_body,
        grid=(5,),
        in_specs=[
            pl.BlockSpec((rows, depth), lambda i: (0, 0)),
            by_column(depth),
            by_column(rows),
            by_column(1),
        ],
        out_specs=[by_column(rows // 2), by_column(rows // 2), by_column(1)],
        out_shape=[
            jax.ShapeDtypeStruct((rows // 2, width), jnp.bfloat16),
            jax.ShapeDtypeStruct((rows // 2, width), jnp.bfloat16),
            jax.ShapeDtypeStruct((1, width), jnp.float32),
        ],
        compiler_params=pltpu.CompilerParams(vmem_limit_bytes=24 * 2**20),
        cost_estimate=pl.CostEstimate(
            flops=2 * rows * depth * width, bytes_accessed=7 * 2**20, transcendentals=0
        ),
        name="weight_products",
    )(left, right, weights, gain)


def outgoing_body(kept_ref, taken_ref, extra_ref, out_ref):
    width = kept_ref.shape[1]
    held = out_ref.shape[1]
    total = kept_ref[...].astype(jnp.float32) + taken_ref[...].astype(jnp.float32)
    for block in range(out_ref.shape[0]):
        out_ref[block, :, :width] = total[block * held : (block + 1) * held].astype(jnp.bfloat16)
        out_ref[block, :, width:] = extra_ref[...]


def outgoing_blocks(kept, taken, extra):
    rows, width = kept.shape
    held, more = extra.shape
    step = 32
    by_row = pl.BlockSpec((step, width), lambda i: (i, 0))
    return pl.pallas_call(
        outgoing_body,
        grid=(rows // step,),
        in_specs=[by_row, by_row, pl.BlockSpec((held, more), lambda i: (0, 0))],
        out_specs=pl.BlockSpec((step // held, held, width + more), lambda i: (i, 0, 0)),
        out_shape=jax.ShapeDtypeStruct((rows // held, held, width + more), jnp.bfloat16),
        compiler_params=pltpu.CompilerParams(vmem_limit_bytes=24 * 2**20),
        cost_estimate=pl.CostEstimate(
            flops=rows * width, bytes_accessed=4 * 2**20, transcendentals=0
        ),
        name="outgoing_blocks",
    )(kept, taken, extra)


def local(owner, qkv, grad_out, w_out, layer_scale):
    slots, tokens = qkv.shape[1], qkv.shape[2]
    size, heads, width = w_out.shape
    groups = 8
    run = tokens // groups
    factor = size ** (-0.5)
    rows = size * heads
    core = lax.axis_index("replica") % 2

    dealt = deal(owner, grad_out, slots)

    position = jnp.arange(rows, dtype=jnp.int32)
    e_of = position % 128 // 4 * 4 + 2 * jnp.where(position < 128, 1 - core, core) + position % 4 // 2
    h_of = position % 2
    column = jnp.arange(rows, dtype=jnp.int32)
    by_head = (column[:, None] == (h_of * size + e_of)[None, :]).astype(jnp.bfloat16)
    by_size = (column[:, None] == (e_of * heads + h_of)[None, :]).astype(jnp.bfloat16)

    block = qkv.reshape(3, slots, tokens, heads, size)
    queries, keys_in, values = block[0], block[1], block[2]
    scores = (
        jnp.einsum("mqhe,mkhe->mhqk", queries, keys_in, preferred_element_type=jnp.float32) * factor
    )
    raised = jnp.exp(scores - jnp.max(scores, axis=-1, keepdims=True))
    probs = raised / jnp.sum(raised, axis=-1, keepdims=True)
    probs_low = probs.astype(jnp.bfloat16)
    attended = jnp.einsum(
        "mhqk,mkhe->mqhe", probs_low, values, preferred_element_type=jnp.float32
    ).astype(jnp.bfloat16)
    weights = jnp.einsum(
        "wp,wc->pc",
        by_size,
        w_out.reshape(rows, width),
        preferred_element_type=jnp.float32,
    )
    scaled_weights = (weights * layer_scale).astype(jnp.bfloat16)
    sent_order = jnp.einsum(
        "nw,wp->np",
        attended.reshape(slots * tokens, rows),
        by_head,
        preferred_element_type=jnp.float32,
    ).astype(jnp.bfloat16)
    grouped = sent_order.reshape(slots, groups, run, rows).transpose(1, 0, 2, 3)

    pieces, places = gather_tokens(dealt)
    in_order = grouped[places].reshape(groups * slots * run, rows)
    flat = pieces.reshape(groups * slots * run, width)
    given, kept, scale_part = weight_products(
        in_order.T, flat, weights.astype(jnp.bfloat16), layer_scale[None, :]
    )
    taken = lax.ppermute(given, "replica", replica_step(lambda z, y, c: (z, y, 1 - c)))
    columns = [
        [z * 16 + y * 2 + c for z in range(4) for y in range(8)] for c in range(2)
    ]
    held = rows // 64
    extra = over_chip_and_tensor(scale_part[0]).astype(jnp.bfloat16)
    extra = jnp.pad(extra.reshape(held, width // held), ((0, 0), (0, 96)))
    outgoing = outgoing_blocks(kept, taken, extra)
    arrived = lax.all_to_all(outgoing, "replica", 0, 0, axis_index_groups=columns)
    summed = jnp.sum(arrived.astype(jnp.float32), axis=0)
    grad_w = summed[:, :width].reshape(size // 64, heads, width)
    grad_scale = summed[:, width : width + width // held].reshape(width)

    flat, _ = lax.optimization_barrier((flat, outgoing))
    d_flat = jnp.einsum(
        "nc,wc->nw", flat, scaled_weights, preferred_element_type=jnp.float32
    ).astype(jnp.bfloat16)
    d_heads = jnp.einsum("np,wp->nw", d_flat, by_head, preferred_element_type=jnp.float32)
    d_grouped = d_heads.astype(jnp.bfloat16).reshape(groups, slots, run, rows)
    back = jnp.sum(
        jnp.where(places[None, :] == jnp.arange(groups)[:, None], jnp.arange(groups)[None, :], 0),
        axis=1,
    )
    d_attended = d_grouped[back].transpose(1, 0, 2, 3).reshape(slots, tokens, heads, size)
    d_values = jnp.einsum(
        "mhqk,mqhe->mkhe", probs_low, d_attended, preferred_element_type=jnp.float32
    ).astype(jnp.bfloat16)
    d_probs = jnp.einsum("mqhe,mkhe->mhqk", d_attended, values, preferred_element_type=jnp.float32)
    row_total = jnp.sum(probs * d_probs, axis=-1, keepdims=True)
    d_scores = (probs * (d_probs - row_total) * factor).astype(jnp.bfloat16)
    d_query = jnp.einsum(
        "mhqk,mkhe->mqhe", d_scores, keys_in, preferred_element_type=jnp.float32
    ).astype(jnp.bfloat16)
    d_keys = jnp.einsum(
        "mhqk,mqhe->mkhe", d_scores, queries, preferred_element_type=jnp.float32
    ).astype(jnp.bfloat16)
    grad_qkv = jnp.stack([d_query, d_keys, d_values]).reshape(3, slots, tokens, heads * size)
    return (grad_qkv, grad_w, grad_scale)


def solution(mesh):
    in_specs = (
        P(),
        P(None, "replica", None, "tensor"),
        P("replica", "tensor", None),
        P(None, "tensor", None),
        P(),
    )
    out_specs = (P(None, "replica", None, "tensor"), P("replica", "tensor", None), P())
    return jax.shard_map(local, mesh=mesh, in_specs=in_specs, out_specs=out_specs, check_vma=False)
```

```python
import jax
import jax.numpy as jnp
from jax import lax
from jax.experimental import pallas as pl
from jax.experimental.pallas import tpu as pltpu
from jax.sharding import PartitionSpec as P

N_X = 4


def tensor_step(shift_hi, shift_x):
    pairs = []
    for index in range(8):
        high, x = index // N_X, index % N_X
        pairs.append((index, (high + shift_hi) % 2 * N_X + (x + shift_x) % N_X))
    return pairs


def deal(owner, grad_out, slot_count):
    replicas, part, lanes = 64, 4, 128
    images, tokens, width = grad_out.shape
    parts, runs = tokens // part, width // lanes
    pieces = parts * runs
    ids = jnp.arange(replicas * images, dtype=jnp.int32)
    same = (owner[:, None] == owner[None, :]) & (ids[None, :] < ids[:, None])
    slot_of = owner * slot_count + jnp.sum(same.astype(jnp.int32), axis=1)
    padded = jnp.pad(slot_of.reshape(replicas, images), ((0, 0), (0, 1)), constant_values=-1)
    row_of = (padded[:, :, None] * part + jnp.arange(part, dtype=jnp.int32)).reshape(-1)
    rows = jnp.arange(replicas * slot_count * part, dtype=jnp.int32)
    chosen = (rows[:, None] == row_of[None, :]).astype(grad_out.dtype)

    spread = grad_out.reshape(images, parts, part, runs, lanes).transpose(3, 1, 0, 2, 4)
    spread = spread.reshape(pieces, images * part, lanes)
    spread = jnp.pad(spread, ((0, replicas - pieces), (0, part), (0, 0)))
    held = lax.all_to_all(spread, "replica", 0, 0).reshape(replicas * (images + 1) * part, lanes)
    dealt = jnp.einsum("mi,ic->mc", chosen, held, preferred_element_type=jnp.float32)
    dealt = dealt.astype(grad_out.dtype).reshape(replicas, slot_count * part, lanes)
    mine = lax.all_to_all(dealt, "replica", 0, 0)[:pieces]
    mine = mine.reshape(runs, parts, slot_count, part, lanes).transpose(2, 1, 3, 0, 4)
    return mine.reshape(slot_count, tokens, width)


def ring_gather(block):
    steps = [lax.ppermute(block, "tensor", tensor_step(0, k)) for k in (1, -1, 2)]
    return [block] + steps


def gather_tokens(block):
    other = lax.ppermute(block, "tensor", tensor_step(1, 0))
    near = ring_gather(block)
    far = ring_gather(other)
    me = lax.axis_index("tensor")
    high, x = me // N_X, me % N_X
    places = []
    for hi in (high, 1 - high):
        for step in (0, -1, 1, 2):
            places.append(hi * N_X + (x + step + N_X) % N_X)
    return jnp.stack(near + far), jnp.stack(places)


def replica_step(move):
    pairs = []
    for index in range(64):
        z, y, core = index // 16, index // 2 % 8, index % 2
        new_z, new_y, new_core = move(z, y, core)
        pairs.append((index, new_z * 16 + new_y * 2 + new_core))
    return pairs


def over_chip_and_tensor(part):
    near = [
        [(chip * 2 + core) * 8 + index for core in range(2) for index in range(8)]
        for chip in range(32)
    ]
    copies = jnp.broadcast_to(part, (16, 1) + part.shape)
    arrived = lax.all_to_all(copies, ("replica", "tensor"), 0, 0, axis_index_groups=near)
    return jnp.sum(arrived, axis=(0, 1))


def product_body(left_ref, right_ref, weight_ref, gain_ref, given_ref, kept_ref, scale_ref):
    product = jnp.dot(left_ref[...], right_ref[...], preferred_element_type=jnp.float32)
    scale_ref[...] = jnp.sum(
        product * weight_ref[...].astype(jnp.float32), axis=0, keepdims=True
    )
    partial = product * gain_ref[...]
    half = given_ref.shape[0]
    given_ref[...] = partial[:half].astype(jnp.bfloat16)
    kept_ref[...] = partial[half:].astype(jnp.bfloat16)


def weight_products(left, right, weights, gain):
    rows, depth = left.shape
    width = right.shape[1]
    step = width // 5
    by_column = lambda height: pl.BlockSpec((height, step), lambda i: (0, i))
    return pl.pallas_call(
        product_body,
        grid=(5,),
        in_specs=[
            pl.BlockSpec((rows, depth), lambda i: (0, 0)),
            by_column(depth),
            by_column(rows),
            by_column(1),
        ],
        out_specs=[by_column(rows // 2), by_column(rows // 2), by_column(1)],
        out_shape=[
            jax.ShapeDtypeStruct((rows // 2, width), jnp.bfloat16),
            jax.ShapeDtypeStruct((rows // 2, width), jnp.bfloat16),
            jax.ShapeDtypeStruct((1, width), jnp.float32),
        ],
        compiler_params=pltpu.CompilerParams(vmem_limit_bytes=24 * 2**20),
        cost_estimate=pl.CostEstimate(
            flops=2 * rows * depth * width, bytes_accessed=7 * 2**20, transcendentals=0
        ),
        name="weight_products",
    )(left, right, weights, gain)


def outgoing_body(kept_ref, taken_ref, extra_ref, out_ref):
    width = kept_ref.shape[1]
    held = out_ref.shape[1]
    for begin in range(0, width, 640):
        columns = slice(begin, begin + 640)
        total = kept_ref[:, columns].astype(jnp.float32) + taken_ref[:, columns].astype(jnp.float32)
        for block in range(out_ref.shape[0]):
            rows = total[block * held : (block + 1) * held]
            out_ref[block, :, columns] = rows.astype(jnp.bfloat16)
    for block in range(out_ref.shape[0]):
        out_ref[block, :, width:] = extra_ref[...]


def outgoing_blocks(kept, taken, extra):
    rows, width = kept.shape
    held, more = extra.shape
    step = 64
    by_row = pl.BlockSpec((step, width), lambda i: (i, 0))
    return pl.pallas_call(
        outgoing_body,
        grid=(rows // step,),
        in_specs=[by_row, by_row, pl.BlockSpec((held, more), lambda i: (0, 0))],
        out_specs=pl.BlockSpec((step // held, held, width + more), lambda i: (i, 0, 0)),
        out_shape=jax.ShapeDtypeStruct((rows // held, held, width + more), jnp.bfloat16),
        compiler_params=pltpu.CompilerParams(vmem_limit_bytes=24 * 2**20),
        cost_estimate=pl.CostEstimate(
            flops=rows * width, bytes_accessed=4 * 2**20, transcendentals=0
        ),
        name="outgoing_blocks",
    )(kept, taken, extra)


def local(owner, qkv, grad_out, w_out, layer_scale):
    slots, tokens = qkv.shape[1], qkv.shape[2]
    size, heads, width = w_out.shape
    groups = 8
    run = tokens // groups
    factor = size ** (-0.5)
    rows = size * heads
    core = lax.axis_index("replica") % 2

    dealt = deal(owner, grad_out, slots)

    position = jnp.arange(rows, dtype=jnp.int32)
    e_of = position % 128 // 4 * 4 + 2 * jnp.where(position < 128, 1 - core, core) + position % 4 // 2
    h_of = position % 2
    column = jnp.arange(rows, dtype=jnp.int32)
    by_head = (column[:, None] == (h_of * size + e_of)[None, :]).astype(jnp.bfloat16)
    by_size = (column[:, None] == (e_of * heads + h_of)[None, :]).astype(jnp.bfloat16)

    block = qkv.reshape(3, slots, tokens, heads, size)
    queries, keys_in, values = block[0], block[1], block[2]
    scores = (
        jnp.einsum("mqhe,mkhe->mhqk", queries, keys_in, preferred_element_type=jnp.float32) * factor
    )
    raised = jnp.exp(scores - jnp.max(scores, axis=-1, keepdims=True))
    probs = raised / jnp.sum(raised, axis=-1, keepdims=True)
    probs_low = probs.astype(jnp.bfloat16)
    attended = jnp.einsum(
        "mhqk,mkhe->mqhe", probs_low, values, preferred_element_type=jnp.float32
    ).astype(jnp.bfloat16)
    weights = jnp.einsum(
        "wp,wc->pc",
        by_size,
        w_out.reshape(rows, width),
        preferred_element_type=jnp.float32,
    )
    scaled_weights = (weights * layer_scale).astype(jnp.bfloat16)
    sent_order = jnp.einsum(
        "nw,wp->np",
        attended.reshape(slots * tokens, rows),
        by_head,
        preferred_element_type=jnp.float32,
    ).astype(jnp.bfloat16)
    grouped = sent_order.reshape(slots, groups, run, rows).transpose(1, 0, 2, 3)

    pieces, places = gather_tokens(dealt)
    in_order = grouped[places].reshape(groups * slots * run, rows)
    flat = pieces.reshape(groups * slots * run, width)
    given, kept, scale_part = weight_products(
        in_order.T, flat, weights.astype(jnp.bfloat16), layer_scale[None, :]
    )
    taken = lax.ppermute(given, "replica", replica_step(lambda z, y, c: (z, y, 1 - c)))
    columns = [
        [z * 16 + y * 2 + c for z in range(4) for y in range(8)] for c in range(2)
    ]
    held = rows // 64
    extra = over_chip_and_tensor(scale_part[0]).astype(jnp.bfloat16)
    extra = jnp.pad(extra.reshape(held, width // held), ((0, 0), (0, 96)))
    outgoing = outgoing_blocks(kept, taken, extra)
    arrived = lax.all_to_all(outgoing, "replica", 0, 0, axis_index_groups=columns)
    summed = jnp.sum(arrived.astype(jnp.float32), axis=0)
    grad_w = summed[:, :width].reshape(size // 64, heads, width)
    grad_scale = summed[:, width : width + width // held].reshape(width)

    flat, _ = lax.optimization_barrier((flat, outgoing))
    d_flat = jnp.einsum(
        "nc,wc->nw", flat, scaled_weights, preferred_element_type=jnp.float32
    ).astype(jnp.bfloat16)
    d_heads = jnp.einsum("np,wp->nw", d_flat, by_head, preferred_element_type=jnp.float32)
    d_grouped = d_heads.astype(jnp.bfloat16).reshape(groups, slots, run, rows)
    back = jnp.sum(
        jnp.where(places[None, :] == jnp.arange(groups)[:, None], jnp.arange(groups)[None, :], 0),
        axis=1,
    )
    d_attended = d_grouped[back].transpose(1, 0, 2, 3).reshape(slots, tokens, heads, size)
    d_values = jnp.einsum(
        "mhqk,mqhe->mkhe", probs_low, d_attended, preferred_element_type=jnp.float32
    ).astype(jnp.bfloat16)
    d_probs = jnp.einsum("mqhe,mkhe->mhqk", d_attended, values, preferred_element_type=jnp.float32)
    row_total = jnp.sum(probs * d_probs, axis=-1, keepdims=True)
    d_scores = (probs * (d_probs - row_total) * factor).astype(jnp.bfloat16)
    d_query = jnp.einsum(
        "mhqk,mkhe->mqhe", d_scores, keys_in, preferred_element_type=jnp.float32
    ).astype(jnp.bfloat16)
    d_keys = jnp.einsum(
        "mhqk,mqhe->mkhe", d_scores, queries, preferred_element_type=jnp.float32
    ).astype(jnp.bfloat16)
    grad_qkv = jnp.stack([d_query, d_keys, d_values]).reshape(3, slots, tokens, heads * size)
    return (grad_qkv, grad_w, grad_scale)


def solution(mesh):
    in_specs = (
        P(),
        P(None, "replica", None, "tensor"),
        P("replica", "tensor", None),
        P(None, "tensor", None),
        P(),
    )
    out_specs = (P(None, "replica", None, "tensor"), P("replica", "tensor", None), P())
    return jax.shard_map(local, mesh=mesh, in_specs=in_specs, out_specs=out_specs, check_vma=False)
```

```python
import jax
import jax.numpy as jnp
from jax import lax
from jax.experimental import pallas as pl
from jax.experimental.pallas import tpu as pltpu
from jax.sharding import PartitionSpec as P

N_X = 4


def tensor_step(shift_hi, shift_x):
    pairs = []
    for index in range(8):
        high, x = index // N_X, index % N_X
        pairs.append((index, (high + shift_hi) % 2 * N_X + (x + shift_x) % N_X))
    return pairs


def deal(owner, grad_out, slot_count):
    replicas, part, lanes = 64, 4, 128
    images, tokens, width = grad_out.shape
    parts, runs = tokens // part, width // lanes
    pieces = parts * runs
    ids = jnp.arange(replicas * images, dtype=jnp.int32)
    same = (owner[:, None] == owner[None, :]) & (ids[None, :] < ids[:, None])
    slot_of = owner * slot_count + jnp.sum(same.astype(jnp.int32), axis=1)
    padded = jnp.pad(slot_of.reshape(replicas, images), ((0, 0), (0, 1)), constant_values=-1)
    row_of = (padded[:, :, None] * part + jnp.arange(part, dtype=jnp.int32)).reshape(-1)
    rows = jnp.arange(replicas * slot_count * part, dtype=jnp.int32)
    chosen = (rows[:, None] == row_of[None, :]).astype(grad_out.dtype)

    spread = grad_out.reshape(images, parts, part, runs, lanes).transpose(3, 1, 0, 2, 4)
    spread = spread.reshape(pieces, images * part, lanes)
    spread = jnp.pad(spread, ((0, replicas - pieces), (0, part), (0, 0)))
    held = lax.all_to_all(spread, "replica", 0, 0).reshape(replicas * (images + 1) * part, lanes)
    dealt = jnp.einsum("mi,ic->mc", chosen, held, preferred_element_type=jnp.float32)
    dealt = dealt.astype(grad_out.dtype).reshape(replicas, slot_count * part, lanes)
    mine = lax.all_to_all(dealt, "replica", 0, 0)[:pieces]
    mine = mine.reshape(runs, parts, slot_count, part, lanes).transpose(2, 1, 3, 0, 4)
    return mine.reshape(slot_count, tokens, width)


def ring_gather(block):
    steps = [lax.ppermute(block, "tensor", tensor_step(0, k)) for k in (1, -1, 2)]
    return [block] + steps


def gather_tokens(block):
    other = lax.ppermute(block, "tensor", tensor_step(1, 0))
    near = ring_gather(block)
    far = ring_gather(other)
    me = lax.axis_index("tensor")
    high, x = me // N_X, me % N_X
    places = []
    for hi in (high, 1 - high):
        for step in (0, -1, 1, 2):
            places.append(hi * N_X + (x + step + N_X) % N_X)
    return jnp.stack(near + far), jnp.stack(places)


def replica_step(move):
    pairs = []
    for index in range(64):
        z, y, core = index // 16, index // 2 % 8, index % 2
        new_z, new_y, new_core = move(z, y, core)
        pairs.append((index, new_z * 16 + new_y * 2 + new_core))
    return pairs


def over_chip_and_tensor(part):
    near = [
        [(chip * 2 + core) * 8 + index for core in range(2) for index in range(8)]
        for chip in range(32)
    ]
    copies = jnp.broadcast_to(part, (16, 1) + part.shape)
    return lax.all_to_all(copies, ("replica", "tensor"), 0, 0, axis_index_groups=near)


def product_body(left_ref, right_ref, weight_ref, gain_ref, given_ref, kept_ref, scale_ref):
    product = jnp.dot(left_ref[...], right_ref[...], preferred_element_type=jnp.float32)
    scale_ref[...] = jnp.sum(
        product * weight_ref[...].astype(jnp.float32), axis=0, keepdims=True
    )
    partial = product * gain_ref[...]
    half = given_ref.shape[0]
    given_ref[...] = partial[:half].astype(jnp.bfloat16)
    kept_ref[...] = partial[half:].astype(jnp.bfloat16)


def weight_products(left, right, weights, gain):
    rows, depth = left.shape
    width = right.shape[1]
    step = width // 5
    by_column = lambda height: pl.BlockSpec((height, step), lambda i: (0, i))
    return pl.pallas_call(
        product_body,
        grid=(5,),
        in_specs=[
            pl.BlockSpec((rows, depth), lambda i: (0, 0)),
            by_column(depth),
            by_column(rows),
            by_column(1),
        ],
        out_specs=[by_column(rows // 2), by_column(rows // 2), by_column(1)],
        out_shape=[
            jax.ShapeDtypeStruct((rows // 2, width), jnp.bfloat16),
            jax.ShapeDtypeStruct((rows // 2, width), jnp.bfloat16),
            jax.ShapeDtypeStruct((1, width), jnp.float32),
        ],
        compiler_params=pltpu.CompilerParams(vmem_limit_bytes=24 * 2**20),
        cost_estimate=pl.CostEstimate(
            flops=2 * rows * depth * width, bytes_accessed=7 * 2**20, transcendentals=0
        ),
        name="weight_products",
    )(left, right, weights, gain)


def outgoing_body(kept_ref, taken_ref, terms_ref, out_ref):
    width = kept_ref.shape[1]
    held = out_ref.shape[1]
    more = out_ref.shape[2] - width
    for begin in range(0, width, 640):
        columns = slice(begin, begin + 640)
        total = kept_ref[:, columns].astype(jnp.float32) + taken_ref[:, columns].astype(jnp.float32)
        for block in range(out_ref.shape[0]):
            rows = total[block * held : (block + 1) * held]
            out_ref[block, :, columns] = rows.astype(jnp.bfloat16)
    terms = jnp.sum(terms_ref[...], axis=0)
    rows = [terms[:, row * more : min((row + 1) * more, width)] for row in range(held)]
    empty = jnp.zeros((1, held * more - width), jnp.float32)
    rows[-1] = jnp.concatenate([rows[-1], empty], axis=1)
    extra = jnp.concatenate(rows).astype(jnp.bfloat16)
    for block in range(out_ref.shape[0]):
        out_ref[block, :, width:] = extra


def outgoing_blocks(kept, taken, terms, held):
    rows, width = kept.shape
    more = -(-width // (held * 128)) * 128
    step = 64
    by_row = pl.BlockSpec((step, width), lambda i: (i, 0))
    return pl.pallas_call(
        outgoing_body,
        grid=(rows // step,),
        in_specs=[by_row, by_row, pl.BlockSpec(terms.shape, lambda i: (0, 0, 0))],
        out_specs=pl.BlockSpec((step // held, held, width + more), lambda i: (i, 0, 0)),
        out_shape=jax.ShapeDtypeStruct((rows // held, held, width + more), jnp.bfloat16),
        compiler_params=pltpu.CompilerParams(vmem_limit_bytes=24 * 2**20),
        cost_estimate=pl.CostEstimate(
            flops=rows * width, bytes_accessed=4 * 2**20, transcendentals=0
        ),
        name="outgoing_blocks",
    )(kept, taken, terms)


def local(owner, qkv, grad_out, w_out, layer_scale):
    slots, tokens = qkv.shape[1], qkv.shape[2]
    size, heads, width = w_out.shape
    groups = 8
    run = tokens // groups
    factor = size ** (-0.5)
    rows = size * heads
    core = lax.axis_index("replica") % 2

    dealt = deal(owner, grad_out, slots)

    position = jnp.arange(rows, dtype=jnp.int32)
    e_of = position % 128 // 4 * 4 + 2 * jnp.where(position < 128, 1 - core, core) + position % 4 // 2
    h_of = position % 2
    column = jnp.arange(rows, dtype=jnp.int32)
    by_head = (column[:, None] == (h_of * size + e_of)[None, :]).astype(jnp.bfloat16)
    by_size = (column[:, None] == (e_of * heads + h_of)[None, :]).astype(jnp.bfloat16)

    block = qkv.reshape(3, slots, tokens, heads, size)
    queries, keys_in, values = block[0], block[1], block[2]
    scores = (
        jnp.einsum("mqhe,mkhe->mhqk", queries, keys_in, preferred_element_type=jnp.float32) * factor
    )
    raised = jnp.exp(scores - jnp.max(scores, axis=-1, keepdims=True))
    probs = raised / jnp.sum(raised, axis=-1, keepdims=True)
    probs_low = probs.astype(jnp.bfloat16)
    attended = jnp.einsum(
        "mhqk,mkhe->mqhe", probs_low, values, preferred_element_type=jnp.float32
    ).astype(jnp.bfloat16)
    weights = jnp.einsum(
        "wp,wc->pc",
        by_size,
        w_out.reshape(rows, width),
        preferred_element_type=jnp.float32,
    )
    scaled_weights = (weights * layer_scale).astype(jnp.bfloat16)
    sent_order = jnp.einsum(
        "nw,wp->np",
        attended.reshape(slots * tokens, rows),
        by_head,
        preferred_element_type=jnp.float32,
    ).astype(jnp.bfloat16)
    grouped = sent_order.reshape(slots, groups, run, rows).transpose(1, 0, 2, 3)

    pieces, places = gather_tokens(dealt)
    in_order = grouped[places].reshape(groups * slots * run, rows)
    flat = pieces.reshape(groups * slots * run, width)
    given, kept, scale_part = weight_products(
        in_order.T, flat, weights.astype(jnp.bfloat16), layer_scale[None, :]
    )
    taken = lax.ppermute(given, "replica", replica_step(lambda z, y, c: (z, y, 1 - c)))
    columns = [
        [z * 16 + y * 2 + c for z in range(4) for y in range(8)] for c in range(2)
    ]
    held = rows // 64
    outgoing = outgoing_blocks(kept, taken, over_chip_and_tensor(scale_part[0]), held)
    arrived = lax.all_to_all(outgoing, "replica", 0, 0, axis_index_groups=columns)
    summed = jnp.sum(arrived.astype(jnp.float32), axis=0)
    grad_w = summed[:, :width].reshape(size // 64, heads, width)
    grad_scale = summed[:, width:].reshape(-1)[:width]

    flat, _ = lax.optimization_barrier((flat, outgoing))
    d_flat = jnp.einsum(
        "nc,wc->nw", flat, scaled_weights, preferred_element_type=jnp.float32
    ).astype(jnp.bfloat16)
    d_heads = jnp.einsum("np,wp->nw", d_flat, by_head, preferred_element_type=jnp.float32)
    d_grouped = d_heads.astype(jnp.bfloat16).reshape(groups, slots, run, rows)
    back = jnp.sum(
        jnp.where(places[None, :] == jnp.arange(groups)[:, None], jnp.arange(groups)[None, :], 0),
        axis=1,
    )
    d_attended = d_grouped[back].transpose(1, 0, 2, 3).reshape(slots, tokens, heads, size)
    d_values = jnp.einsum(
        "mhqk,mqhe->mkhe", probs_low, d_attended, preferred_element_type=jnp.float32
    ).astype(jnp.bfloat16)
    d_probs = jnp.einsum("mqhe,mkhe->mhqk", d_attended, values, preferred_element_type=jnp.float32)
    row_total = jnp.sum(probs * d_probs, axis=-1, keepdims=True)
    d_scores = (probs * (d_probs - row_total) * factor).astype(jnp.bfloat16)
    d_query = jnp.einsum(
        "mhqk,mkhe->mqhe", d_scores, keys_in, preferred_element_type=jnp.float32
    ).astype(jnp.bfloat16)
    d_keys = jnp.einsum(
        "mhqk,mqhe->mkhe", d_scores, queries, preferred_element_type=jnp.float32
    ).astype(jnp.bfloat16)
    grad_qkv = jnp.stack([d_query, d_keys, d_values]).reshape(3, slots, tokens, heads * size)
    return (grad_qkv, grad_w, grad_scale)


def solution(mesh):
    in_specs = (
        P(),
        P(None, "replica", None, "tensor"),
        P("replica", "tensor", None),
        P(None, "tensor", None),
        P(),
    )
    out_specs = (P(None, "replica", None, "tensor"), P("replica", "tensor", None), P())
    return jax.shard_map(local, mesh=mesh, in_specs=in_specs, out_specs=out_specs, check_vma=False)
```

```python
import jax
import jax.numpy as jnp
from jax import lax
from jax.experimental import pallas as pl
from jax.experimental.pallas import tpu as pltpu
from jax.sharding import PartitionSpec as P

N_X = 4


def tensor_step(shift_hi, shift_x):
    pairs = []
    for index in range(8):
        high, x = index // N_X, index % N_X
        pairs.append((index, (high + shift_hi) % 2 * N_X + (x + shift_x) % N_X))
    return pairs


def spread_body(image_ref, out_ref):
    images, tokens, width = image_ref.shape
    part, lanes = 4, 128
    empty = jnp.zeros((part, lanes), jnp.float32)
    for run in range(width // lanes):
        tiles = [
            image_ref[image, :, run * lanes : (run + 1) * lanes].astype(jnp.float32)
            for image in range(images)
        ]
        for index in range(tokens // part):
            rows = [tile[index * part : (index + 1) * part] for tile in tiles] + [empty]
            piece = run * (tokens // part) + index
            out_ref[piece] = jnp.concatenate(rows).astype(jnp.bfloat16)
    used = width // lanes * (tokens // part)
    out_ref[used:] = jnp.zeros((out_ref.shape[0] - used,) + out_ref.shape[1:], jnp.bfloat16)


def spread_pieces(grad_out, replicas):
    rows = 4 * (grad_out.shape[0] + 1)
    return pl.pallas_call(
        spread_body,
        out_shape=jax.ShapeDtypeStruct((replicas, rows, 128), grad_out.dtype),
        cost_estimate=pl.CostEstimate(flops=0, bytes_accessed=2**19, transcendentals=0),
        name="spread_pieces",
    )(grad_out)


def deal(owner, grad_out, slot_count):
    replicas, part, lanes = 64, 4, 128
    images, tokens, width = grad_out.shape
    parts, runs = tokens // part, width // lanes
    pieces = parts * runs
    ids = jnp.arange(replicas * images, dtype=jnp.int32)
    same = (owner[:, None] == owner[None, :]) & (ids[None, :] < ids[:, None])
    slot_of = owner * slot_count + jnp.sum(same.astype(jnp.int32), axis=1)
    padded = jnp.pad(slot_of.reshape(replicas, images), ((0, 0), (0, 1)), constant_values=-1)
    row_of = (padded[:, :, None] * part + jnp.arange(part, dtype=jnp.int32)).reshape(-1)
    rows = jnp.arange(replicas * slot_count * part, dtype=jnp.int32)
    chosen = (rows[:, None] == row_of[None, :]).astype(grad_out.dtype)

    spread = spread_pieces(grad_out, replicas)
    held = lax.all_to_all(spread, "replica", 0, 0).reshape(replicas * (images + 1) * part, lanes)
    dealt = jnp.einsum("mi,ic->mc", chosen, held, preferred_element_type=jnp.float32)
    dealt = dealt.astype(grad_out.dtype).reshape(replicas, slot_count * part, lanes)
    mine = lax.all_to_all(dealt, "replica", 0, 0)[:pieces]
    mine = mine.reshape(runs, parts, slot_count, part, lanes).transpose(2, 1, 3, 0, 4)
    return mine.reshape(slot_count, tokens, width)


def ring_gather(block):
    steps = [lax.ppermute(block, "tensor", tensor_step(0, k)) for k in (1, -1, 2)]
    return [block] + steps


def gather_tokens(block):
    other = lax.ppermute(block, "tensor", tensor_step(1, 0))
    near = ring_gather(block)
    far = ring_gather(other)
    me = lax.axis_index("tensor")
    high, x = me // N_X, me % N_X
    places = []
    for hi in (high, 1 - high):
        for step in (0, -1, 1, 2):
            places.append(hi * N_X + (x + step + N_X) % N_X)
    return jnp.stack(near + far), jnp.stack(places)


def replica_step(move):
    pairs = []
    for index in range(64):
        z, y, core = index // 16, index // 2 % 8, index % 2
        new_z, new_y, new_core = move(z, y, core)
        pairs.append((index, new_z * 16 + new_y * 2 + new_core))
    return pairs


def over_chip_and_tensor(part):
    near = [
        [(chip * 2 + core) * 8 + index for core in range(2) for index in range(8)]
        for chip in range(32)
    ]
    copies = jnp.broadcast_to(part, (16, 1) + part.shape)
    return lax.all_to_all(copies, ("replica", "tensor"), 0, 0, axis_index_groups=near)


def product_body(left_ref, right_ref, weight_ref, gain_ref, given_ref, kept_ref, scale_ref):
    product = jnp.dot(left_ref[...], right_ref[...], preferred_element_type=jnp.float32)
    scale_ref[...] = jnp.sum(
        product * weight_ref[...].astype(jnp.float32), axis=0, keepdims=True
    )
    partial = product * gain_ref[...]
    half = given_ref.shape[0]
    given_ref[...] = partial[:half].astype(jnp.bfloat16)
    kept_ref[...] = partial[half:].astype(jnp.bfloat16)


def weight_products(left, right, weights, gain):
    rows, depth = left.shape
    width = right.shape[1]
    step = width // 5
    by_column = lambda height: pl.BlockSpec((height, step), lambda i: (0, i))
    return pl.pallas_call(
        product_body,
        grid=(5,),
        in_specs=[
            pl.BlockSpec((rows, depth), lambda i: (0, 0)),
            by_column(depth),
            by_column(rows),
            by_column(1),
        ],
        out_specs=[by_column(rows // 2), by_column(rows // 2), by_column(1)],
        out_shape=[
            jax.ShapeDtypeStruct((rows // 2, width), jnp.bfloat16),
            jax.ShapeDtypeStruct((rows // 2, width), jnp.bfloat16),
            jax.ShapeDtypeStruct((1, width), jnp.float32),
        ],
        compiler_params=pltpu.CompilerParams(vmem_limit_bytes=24 * 2**20),
        cost_estimate=pl.CostEstimate(
            flops=2 * rows * depth * width, bytes_accessed=7 * 2**20, transcendentals=0
        ),
        name="weight_products",
    )(left, right, weights, gain)


def outgoing_body(kept_ref, taken_ref, terms_ref, out_ref):
    width = kept_ref.shape[1]
    held = out_ref.shape[1]
    more = out_ref.shape[2] - width
    for begin in range(0, width, 640):
        columns = slice(begin, begin + 640)
        total = kept_ref[:, columns].astype(jnp.float32) + taken_ref[:, columns].astype(jnp.float32)
        for block in range(out_ref.shape[0]):
            rows = total[block * held : (block + 1) * held]
            out_ref[block, :, columns] = rows.astype(jnp.bfloat16)
    terms = jnp.sum(terms_ref[...], axis=0)
    rows = [terms[:, row * more : min((row + 1) * more, width)] for row in range(held)]
    empty = jnp.zeros((1, held * more - width), jnp.float32)
    rows[-1] = jnp.concatenate([rows[-1], empty], axis=1)
    extra = jnp.concatenate(rows).astype(jnp.bfloat16)
    for block in range(out_ref.shape[0]):
        out_ref[block, :, width:] = extra


def outgoing_blocks(kept, taken, terms, held):
    rows, width = kept.shape
    more = -(-width // (held * 128)) * 128
    step = 64
    by_row = pl.BlockSpec((step, width), lambda i: (i, 0))
    return pl.pallas_call(
        outgoing_body,
        grid=(rows // step,),
        in_specs=[by_row, by_row, pl.BlockSpec(terms.shape, lambda i: (0, 0, 0))],
        out_specs=pl.BlockSpec((step // held, held, width + more), lambda i: (i, 0, 0)),
        out_shape=jax.ShapeDtypeStruct((rows // held, held, width + more), jnp.bfloat16),
        compiler_params=pltpu.CompilerParams(vmem_limit_bytes=24 * 2**20),
        cost_estimate=pl.CostEstimate(
            flops=rows * width, bytes_accessed=4 * 2**20, transcendentals=0
        ),
        name="outgoing_blocks",
    )(kept, taken, terms)


def local(owner, qkv, grad_out, w_out, layer_scale):
    slots, tokens = qkv.shape[1], qkv.shape[2]
    size, heads, width = w_out.shape
    groups = 8
    run = tokens // groups
    factor = size ** (-0.5)
    rows = size * heads
    core = lax.axis_index("replica") % 2

    dealt = deal(owner, grad_out, slots)

    position = jnp.arange(rows, dtype=jnp.int32)
    e_of = position % 128 // 4 * 4 + 2 * jnp.where(position < 128, 1 - core, core) + position % 4 // 2
    h_of = position % 2
    column = jnp.arange(rows, dtype=jnp.int32)
    by_head = (column[:, None] == (h_of * size + e_of)[None, :]).astype(jnp.bfloat16)
    by_size = (column[:, None] == (e_of * heads + h_of)[None, :]).astype(jnp.bfloat16)

    block = qkv.reshape(3, slots, tokens, heads, size)
    queries, keys_in, values = block[0], block[1], block[2]
    scores = (
        jnp.einsum("mqhe,mkhe->mhqk", queries, keys_in, preferred_element_type=jnp.float32) * factor
    )
    raised = jnp.exp(scores - jnp.max(scores, axis=-1, keepdims=True))
    probs = raised / jnp.sum(raised, axis=-1, keepdims=True)
    probs_low = probs.astype(jnp.bfloat16)
    attended = jnp.einsum(
        "mhqk,mkhe->mqhe", probs_low, values, preferred_element_type=jnp.float32
    ).astype(jnp.bfloat16)
    weights = jnp.einsum(
        "wp,wc->pc",
        by_size,
        w_out.reshape(rows, width),
        preferred_element_type=jnp.float32,
    )
    scaled_weights = (weights * layer_scale).astype(jnp.bfloat16)
    sent_order = jnp.einsum(
        "nw,wp->np",
        attended.reshape(slots * tokens, rows),
        by_head,
        preferred_element_type=jnp.float32,
    ).astype(jnp.bfloat16)
    grouped = sent_order.reshape(slots, groups, run, rows).transpose(1, 0, 2, 3)

    pieces, places = gather_tokens(dealt)
    in_order = grouped[places].reshape(groups * slots * run, rows)
    flat = pieces.reshape(groups * slots * run, width)
    given, kept, scale_part = weight_products(
        in_order.T, flat, weights.astype(jnp.bfloat16), layer_scale[None, :]
    )
    taken = lax.ppermute(given, "replica", replica_step(lambda z, y, c: (z, y, 1 - c)))
    columns = [
        [z * 16 + y * 2 + c for z in range(4) for y in range(8)] for c in range(2)
    ]
    held = rows // 64
    outgoing = outgoing_blocks(kept, taken, over_chip_and_tensor(scale_part[0]), held)
    arrived = lax.all_to_all(outgoing, "replica", 0, 0, axis_index_groups=columns)
    summed = jnp.sum(arrived.astype(jnp.float32), axis=0)
    grad_w = summed[:, :width].reshape(size // 64, heads, width)
    grad_scale = summed[:, width:].reshape(-1)[:width]

    flat, _ = lax.optimization_barrier((flat, outgoing))
    d_flat = jnp.einsum(
        "nc,wc->nw", flat, scaled_weights, preferred_element_type=jnp.float32
    ).astype(jnp.bfloat16)
    d_heads = jnp.einsum("np,wp->nw", d_flat, by_head, preferred_element_type=jnp.float32)
    d_grouped = d_heads.astype(jnp.bfloat16).reshape(groups, slots, run, rows)
    back = jnp.sum(
        jnp.where(places[None, :] == jnp.arange(groups)[:, None], jnp.arange(groups)[None, :], 0),
        axis=1,
    )
    d_attended = d_grouped[back].transpose(1, 0, 2, 3).reshape(slots, tokens, heads, size)
    d_values = jnp.einsum(
        "mhqk,mqhe->mkhe", probs_low, d_attended, preferred_element_type=jnp.float32
    ).astype(jnp.bfloat16)
    d_probs = jnp.einsum("mqhe,mkhe->mhqk", d_attended, values, preferred_element_type=jnp.float32)
    row_total = jnp.sum(probs * d_probs, axis=-1, keepdims=True)
    d_scores = (probs * (d_probs - row_total) * factor).astype(jnp.bfloat16)
    d_query = jnp.einsum(
        "mhqk,mkhe->mqhe", d_scores, keys_in, preferred_element_type=jnp.float32
    ).astype(jnp.bfloat16)
    d_keys = jnp.einsum(
        "mhqk,mqhe->mkhe", d_scores, queries, preferred_element_type=jnp.float32
    ).astype(jnp.bfloat16)
    grad_qkv = jnp.stack([d_query, d_keys, d_values]).reshape(3, slots, tokens, heads * size)
    return (grad_qkv, grad_w, grad_scale)


def solution(mesh):
    in_specs = (
        P(),
        P(None, "replica", None, "tensor"),
        P("replica", "tensor", None),
        P(None, "tensor", None),
        P(),
    )
    out_specs = (P(None, "replica", None, "tensor"), P("replica", "tensor", None), P())
    return jax.shard_map(local, mesh=mesh, in_specs=in_specs, out_specs=out_specs, check_vma=False)
```
